128 devices in a mesh: head: 4 (over y_lo, core), ctx: 32 (over x, y_hi, z).
Axes of the slice: x: 4, y: 4 (y_hi: 2, y_lo: 2; y = y_hi * 2 + y_lo), z: 4, core: 2. Of those that a mesh axis runs over, the one named last changes fastest.
Arguments:
- queries: bfloat16 [16384, 5120], P(('head', 'ctx')), may hold values from -160 to 160
- keys: bfloat16 [16384, 1024], P(('head', 'ctx')), may hold values from -13 to 13
- values: bfloat16 [16384, 1024], P(('head', 'ctx')), may hold values from -6 to 6
- selection: int32 [128, 8], P(('head', 'ctx')), may hold values from 0 to 127, as said below
- seg_lengths: int32 [8], replicated, may hold values from 1 to 8192, 16384 in all
Outputs:
- attended: bfloat16 [16384, 5120], P(('head', 'ctx'))
The draws below stay inside these ranges and needn't reach their ends.
Inputs may be any that keep to these rules, and one draw needn't show every extreme that they name: `selection`: each row b holds 8 different entries, among them b itself. Its entries lie in 8 different classes of entry % 32. An entry greater than b occurs only where its class holds no block up to b.
All inputs are finite; a program needn't handle non-finite values.
Results may differ from the reference program's by a relative error of at most 0.0039.
Values may be sent and summed in bfloat16 or wider, within the bound.
No kernel may reach another device: no remote copies, remote signals or barrier semaphores. Data moves between devices by JAX's collectives and lax.ppermute only.
A program may use at most 128 MiB of HBM per device.

```python
import math
import jax
import jax.numpy as jnp
import numpy as np
from jax import lax

HQ = 40
HK = 8
DH = 128
BLOCK = 128
TOPK = 8
NSEG = 8
TOK_DEV = 128
TOKENS = 16384
NB = 128
N_HEAD = 4
N_CTX = 32


def anchor_rows():
    rows = jnp.arange(TOKENS, dtype=jnp.int32)
    spacing = TOKENS // 8
    anchor = rows % spacing == BLOCK // 2 + 3
    return anchor


def base_keys(key, spread):
    normal = jnp.clip(jax.random.normal(jax.random.fold_in(key, 11), (TOKENS, HK * DH), jnp.float32), -6.0, 6.0)
    level = jax.random.uniform(jax.random.fold_in(key, 12), (TOKENS, 1), jnp.float32, -1.0, 1.0)
    anchor = anchor_rows()
    row_scale = jnp.where(anchor[:, None], 1.0, jnp.exp(spread * level))
    return normal * row_scale


def draw_keys(key, part):
    result = base_keys(key, 0.0)
    return result.astype(jnp.bfloat16)


def draw_queries(key, part):
    key = jax.random.fold_in(key, 2)
    result = jnp.clip(jax.random.normal(key, (TOKENS, HQ * DH), jnp.float32), -6.0, 6.0)
    return result.astype(jnp.bfloat16)


def draw_selection(key, part):
    key = jax.random.fold_in(key, 5)
    per_shard = TOK_DEV // BLOCK
    nblocks = TOKENS // BLOCK
    owned = N_HEAD * per_shard
    rows = jnp.arange(nblocks, dtype=jnp.int32)
    own_owner = rows // per_shard % N_CTX
    classes = jnp.arange(N_CTX, dtype=jnp.int32)
    ranks = jax.random.randint(jax.random.fold_in(key, 1), (nblocks, N_CTX), 0, 1 << 16) * N_CTX + classes[None, :]
    ranks = jnp.where(classes[None, :] == own_owner[:, None], 1 << 30, ranks)
    unused, owners = lax.top_k(ranks, TOPK)
    owners = owners.astype(jnp.int32)
    counter = jnp.arange(owned, dtype=jnp.int32)
    candidates = (counter[None, None, :] // per_shard * N_CTX + owners[:, :, None]) * per_shard + counter[None, None, :] % per_shard
    count = jnp.sum((candidates <= rows[:, None, None]).astype(jnp.int32), axis=-1)
    draws = jax.random.randint(jax.random.fold_in(key, 2), (nblocks, TOPK), 0, 1 << 20)
    which = jnp.where(count > 0, draws % jnp.maximum(count, 1), draws % owned)
    chosen = (which // per_shard * N_CTX + owners) * per_shard + which % per_shard
    return jnp.where(owners == own_owner[:, None], rows[:, None], chosen).astype(jnp.int32)


def block_scale(stream_key, dims, shards, least, high):
    def one(dim, shards_of):
        steps = jax.random.uniform(jax.random.fold_in(jax.random.fold_in(stream_key, 6), dim), (shards_of,), jnp.float32, least / len(shards), high / len(shards))
        return jnp.repeat(jnp.exp(steps), dims[dim] // shards_of).reshape((-1,) + (1,) * (len(dims) - dim - 1))

    factor_of = one(*shards[0])
    for cut in shards[1:]:
        factor_of = factor_of * one(*cut)
    return factor_of


def split_up(amount, total, most, skew):
    portions = [(1 << 20) // math.isqrt(standing ** skew) + 1 for standing in range(2, amount + 1)]
    spare, given = total - most - (amount - 1), [1] * (amount - 1)
    while spare > 0:
        free = [i for i in range(amount - 1) if given[i] < most]
        mass, budget = sum([portions[i] for i in free]), spare
        for i in free:
            addition = min(most - given[i], max(1, budget * portions[i] // mass), spare)
            given[i] = given[i] + addition
            spare = spare - addition
    return np.array([most] + given)


def uneven_parts(key, count, total, bound, slope):
    if count == 2:
        one = jax.random.randint(key, (), max(1, total - bound), min(bound, total - 1) + 1)
        return jnp.stack([one, total - one])
    sizes = jnp.asarray(split_up(count, total, bound, slope), jnp.int32)
    pairs = (count - 1) // 2
    giver, taker = sizes[1:1 + 2 * pairs:2], sizes[2:2 + 2 * pairs:2]
    slack = jnp.minimum(giver - 1, bound - taker)
    shifted = jax.random.randint(jax.random.fold_in(key, 1), (pairs,), 0, 1 << 20) % (slack + 1)
    sizes = sizes.at[1:1 + 2 * pairs:2].set(giver - shifted).at[2:2 + 2 * pairs:2].set(taker + shifted)
    return sizes[jax.random.permutation(jax.random.fold_in(key, 2), count)]


def noise(key, dims, scale, bound, cuts=(), kind=jnp.bfloat16):
    values = jax.random.normal(key, dims, jnp.float32) * scale
    if len(cuts) > 0:
        values = block_scale(key, dims, cuts, -0.22, 0.18) * values
    return jnp.clip(values, min=-bound, max=bound).astype(kind)


def setup_inputs(seed: int = 0) -> dict:
    seeds = jax.random.split(jax.random.key(seed), 6)
    return {
        "queries": draw_queries(jax.random.fold_in(seeds[5], 71), 0),
        "keys": draw_keys(jax.random.fold_in(seeds[5], 71), 0),
        "values": noise(seeds[2], (TOKENS, HK * DH), 1.0, 6.0, ((0, 128),)),
        "selection": draw_selection(jax.random.fold_in(seeds[5], 71), 0),
        "seg_lengths": uneven_parts(seeds[4], NSEG, TOKENS, TOKENS // 2, 2).astype(jnp.int32),
    }


def reference(queries, keys, values, selection, seg_lengths):
    group = HQ // HK
    scale = DH ** -0.5
    ends = jnp.cumsum(seg_lengths).astype(jnp.int32)

    def document(positions):
        return jnp.sum((positions[..., None] >= ends).astype(jnp.int32), axis=-1)

    query_blocks = queries.reshape(NB, BLOCK, HK, group, DH)
    key_blocks = keys.reshape(NB, BLOCK, HK, DH)
    value_blocks = values.reshape(NB, BLOCK, HK, DH)
    offsets = jnp.arange(BLOCK, dtype=jnp.int32)

    def one_block(index):
        picked = selection[index]
        query_now = query_blocks[index].astype(jnp.float32)
        key_now = key_blocks[picked].reshape(TOPK * BLOCK, HK, DH).astype(jnp.float32)
        value_now = value_blocks[picked].reshape(TOPK * BLOCK, HK, DH).astype(jnp.float32)
        query_pos = index * BLOCK + offsets
        key_pos = (picked[:, None] * BLOCK + offsets[None, :]).reshape(-1)
        allowed = (key_pos[None, :] <= query_pos[:, None]) & (document(key_pos)[None, :] == document(query_pos)[:, None])
        scores = jnp.einsum('qhgd,khd->qhgk', query_now, key_now) * scale
        scores = jnp.where(allowed[:, None, None, :], scores, -jnp.inf)
        top = jnp.max(scores, axis=-1, keepdims=True)
        expo = jnp.where(allowed[:, None, None, :], jnp.exp(scores - top), 0.0)
        total = jnp.sum(expo, axis=-1)
        weights = lax.optimization_barrier(expo.astype(jnp.bfloat16)).astype(jnp.float32)
        mixed = jnp.einsum('qhgk,khd->qhgd', weights, value_now) / total[..., None]
        return mixed.astype(jnp.bfloat16)

    result = lax.map(one_block, jnp.arange(NB, dtype=jnp.int32))
    return result.reshape(TOKENS, HQ * DH)
```

```python
import jax
import jax.numpy as jnp
from jax import lax
from jax.experimental import pallas as pl
from jax.experimental.pallas import tpu as pltpu
from jax.sharding import PartitionSpec as P

HQ = 40
HK = 8
DH = 128
BLOCK = 128
TOPK = 8
NSEG = 8
GROUP = HQ // HK
REMOTE = TOPK - 1
DEV = 128
ROWS = 16
PARTS = BLOCK // ROWS
UNITS = 2 * HK
MESSAGE = ROWS + 16
AXES = ("head", "ctx")
SCALE = DH**-0.5
LOG2E = 1.4426950408889634
FILL = -1e30


def remote_picks(sel_ref, me):
    picks = []
    passed = jnp.int32(0)
    for slot in range(REMOTE):
        passed = jnp.where(sel_ref[0, slot] == me, 1, passed)
        picks.append(jnp.where(passed == 1, sel_ref[0, slot + 1], sel_ref[0, slot]))
    return picks


def own_block():
    return lax.axis_index("head") * lax.axis_size("ctx") + lax.axis_index("ctx")


def pack_kernel(sel_ref, k_ref, v_ref, out_ref):
    picks = remote_picks(sel_ref, own_block())
    lane = lax.broadcasted_iota(jnp.int32, (16, BLOCK), 1)
    row = jnp.zeros((16, BLOCK), jnp.int32)
    for slot in range(REMOTE):
        row = jnp.where(lane == slot, picks[slot], row)
    row = row.astype(jnp.float32).astype(jnp.bfloat16)
    for unit in range(UNITS):
        src = k_ref if unit < HK else v_ref
        col = (unit % HK) * DH
        for part in range(PARTS):
            share = unit * PARTS + part
            out_ref[share, :ROWS, :] = src[part * ROWS : (part + 1) * ROWS, col : col + DH]
            out_ref[share, ROWS:, :] = row


def gather_kernel(picks_ref, table_ref, out_ref):
    @pl.loop(0, DEV)
    def _(dest):
        for slot in range(REMOTE):
            block = picks_ref[dest * REMOTE + slot]
            out_ref[dest, slot] = table_ref[block, :ROWS, :]


def attend_kernel(sel_ref, len_ref, q_ref, k_ref, v_ref, got_ref, out_ref, bias_ref):
    me = own_block()
    picks = remote_picks(sel_ref, me)
    row = lax.broadcasted_iota(jnp.int32, (BLOCK, BLOCK), 0) + me * BLOCK
    lane = lax.broadcasted_iota(jnp.int32, (BLOCK, BLOCK), 1)
    start = jnp.zeros((BLOCK, BLOCK), jnp.int32)
    end = jnp.int32(0)
    for seg in range(NSEG):
        end = end + len_ref[seg]
        start = jnp.where(row >= end, end, start)
    for slot, block in enumerate([me] + picks):
        pos = lane + block * BLOCK
        allowed = (pos <= row) & (pos >= start)
        bias_ref[:, slot * BLOCK : (slot + 1) * BLOCK] = jnp.where(allowed, 0.0, FILL)
    for head in range(HK):
        col = head * DH

        def stacked(own, unit):
            parts = [own[:, col : col + DH]]
            for slot in range(REMOTE):
                share = got_ref[unit * PARTS : (unit + 1) * PARTS, slot]
                parts.append(share.reshape(BLOCK, DH))
            return jnp.concatenate(parts, axis=0)

        keys = stacked(k_ref, head)
        vals = stacked(v_ref, HK + head)
        for g in range(GROUP):
            qcol = (head * GROUP + g) * DH
            q = q_ref[:, qcol : qcol + DH]
            s = lax.dot_general(q, keys, (((1,), (1,)), ((), ())), preferred_element_type=jnp.float32)
            s = s + bias_ref[...]
            top = jnp.max(s, axis=1, keepdims=True)
            p = jnp.exp2((s - top) * (SCALE * LOG2E))
            total = jnp.sum(p, axis=1, keepdims=True)
            mixed = jnp.dot(p.astype(jnp.bfloat16), vals, preferred_element_type=jnp.float32)
            out_ref[:, qcol : qcol + DH] = (mixed / total).astype(jnp.bfloat16)


def vmem():
    return pl.BlockSpec(memory_space=pltpu.VMEM)


def smem():
    return pl.BlockSpec(memory_space=pltpu.SMEM)


def params():
    return pltpu.CompilerParams(vmem_limit_bytes=48 * 1024 * 1024)


def body(queries, keys, values, selection, seg_lengths):
    packed = pl.pallas_call(
        pack_kernel,
        out_shape=jax.ShapeDtypeStruct((DEV, MESSAGE, DH), jnp.bfloat16),
        in_specs=[smem(), vmem(), vmem()],
        out_specs=vmem(),
        compiler_params=params(),
        name="pack",
    )(selection, keys, values)
    table = lax.all_to_all(packed, AXES, 0, 0, tiled=True)
    picks = table[:, ROWS, :REMOTE].astype(jnp.int32).reshape(DEV * REMOTE)
    shares = pl.pallas_call(
        gather_kernel,
        out_shape=jax.ShapeDtypeStruct((DEV, REMOTE, ROWS, DH), jnp.bfloat16),
        in_specs=[smem(), vmem()],
        out_specs=vmem(),
        compiler_params=params(),
        name="pick",
    )(picks, table)
    got = lax.all_to_all(shares, AXES, 0, 0, tiled=True)
    return pl.pallas_call(
        attend_kernel,
        out_shape=jax.ShapeDtypeStruct((BLOCK, HQ * DH), jnp.bfloat16),
        in_specs=[smem(), smem(), vmem(), vmem(), vmem(), vmem()],
        out_specs=vmem(),
        scratch_shapes=[pltpu.VMEM((BLOCK, TOPK * BLOCK), jnp.float32)],
        compiler_params=params(),
        name="attend",
    )(selection, seg_lengths, queries, keys, values, got)


def solution(mesh):
    return jax.shard_map(
        body,
        mesh=mesh,
        in_specs=(P(AXES, None), P(AXES, None), P(AXES, None), P(AXES, None), P()),
        out_specs=P(AXES, None),
        check_vma=False,
    )
```

```python
import jax
import jax.numpy as jnp
from jax import lax
from jax.experimental import pallas as pl
from jax.experimental.pallas import tpu as pltpu
from jax.sharding import PartitionSpec as P

HQ = 40
HK = 8
DH = 128
BLOCK = 128
TOPK = 8
NSEG = 8
GROUP = HQ // HK
REMOTE = TOPK - 1
DEV = 128
ROWS = 16
PARTS = BLOCK // ROWS
UNITS = 2 * HK
EXTRA = 8
MESSAGE = ROWS + EXTRA
AXES = ("head", "ctx")
SCALE = DH**-0.5
LOG2E = 1.4426950408889634
FILL = -1e30


def own_block():
    return lax.axis_index("head") * lax.axis_size("ctx") + lax.axis_index("ctx")


def remote_picks(sel_ref, me):
    picks = []
    passed = jnp.int32(0)
    for slot in range(REMOTE):
        passed = jnp.where(sel_ref[0, slot] == me, 1, passed)
        picks.append(jnp.where(passed == 1, sel_ref[0, slot + 1], sel_ref[0, slot]))
    return picks


def pack_kernel(sel_hbm, len_hbm, k_ref, v_ref, out_ref, bias_ref, sel_ref, len_ref, sems):
    scalars = [
        pltpu.make_async_copy(sel_hbm, sel_ref, sems.at[UNITS]),
        pltpu.make_async_copy(len_hbm, len_ref, sems.at[UNITS + 1]),
    ]
    shares = []
    for unit in range(UNITS):
        src = k_ref if unit < HK else v_ref
        col = (unit % HK) * DH
        shares.append(
            pltpu.make_async_copy(
                src.at[:, :, col : col + DH],
                out_ref.at[unit * PARTS : (unit + 1) * PARTS, :ROWS, :],
                sems.at[unit],
            )
        )
    for copy in scalars + shares:
        copy.start()
    for copy in scalars:
        copy.wait()
    me = own_block()
    picks = remote_picks(sel_ref, me)
    lane = lax.broadcasted_iota(jnp.int32, (EXTRA, BLOCK), 1)
    row = jnp.zeros((EXTRA, BLOCK), jnp.int32)
    for slot in range(REMOTE):
        row = jnp.where(lane == slot, picks[slot], row)
    row = row.astype(jnp.float32).astype(jnp.bfloat16)
    for share in range(DEV):
        out_ref[share, ROWS:, :] = row
    row = lax.broadcasted_iota(jnp.int32, (BLOCK, BLOCK), 0) + me * BLOCK
    lane = lax.broadcasted_iota(jnp.int32, (BLOCK, BLOCK), 1)
    start = jnp.zeros((BLOCK, BLOCK), jnp.int32)
    end = jnp.int32(0)
    for seg in range(NSEG):
        end = end + len_ref[seg]
        start = jnp.where(row >= end, end, start)
    for slot, block in enumerate([me] + picks):
        pos = lane + block * BLOCK
        allowed = (pos <= row) & (pos >= start)
        bias_ref[:, slot * BLOCK : (slot + 1) * BLOCK] = jnp.where(allowed, 0.0, FILL)
    for copy in shares:
        copy.wait()


def gather_kernel(picks_ref, table_ref, out_ref):
    @pl.loop(0, DEV, unroll=8)
    def _(dest):
        for slot in range(REMOTE):
            block = picks_ref[dest * REMOTE + slot]
            out_ref[dest, slot] = table_ref[block, :ROWS, :]


def attend_kernel(q_ref, k_ref, v_ref, bias_ref, got_ref, out_ref):
    for head in range(HK):
        col = head * DH

        def stacked(own, unit):
            parts = [own[:, col : col + DH]]
            for slot in range(REMOTE):
                share = got_ref[unit * PARTS : (unit + 1) * PARTS, slot]
                parts.append(share.reshape(BLOCK, DH))
            return jnp.concatenate(parts, axis=0)

        keys = stacked(k_ref, head)
        vals = stacked(v_ref, HK + head)
        ones = jnp.ones((TOPK * BLOCK, DH), jnp.bfloat16)
        vals = jnp.concatenate([vals, ones], axis=1)
        for g in range(GROUP):
            qcol = (head * GROUP + g) * DH
            q = q_ref[:, qcol : qcol + DH]
            s = lax.dot_general(q, keys, (((1,), (1,)), ((), ())), preferred_element_type=jnp.float32)
            s = s + bias_ref[...]
            top = jnp.max(s, axis=1, keepdims=True)
            p = jnp.exp2((s - top) * (SCALE * LOG2E)).astype(jnp.bfloat16)
            mixed = jnp.dot(p, vals, preferred_element_type=jnp.float32)
            out_ref[:, qcol : qcol + DH] = (mixed[:, :DH] / mixed[:, DH:]).astype(jnp.bfloat16)


def vmem():
    return pl.BlockSpec(memory_space=pltpu.VMEM)


def hbm():
    return pl.BlockSpec(memory_space=pltpu.HBM)


def smem():
    return pl.BlockSpec(memory_space=pltpu.SMEM)


def params():
    return pltpu.CompilerParams(vmem_limit_bytes=48 * 1024 * 1024)


def in_hbm(x):
    return pltpu.with_memory_space_constraint(x, pltpu.HBM)


def body(queries, keys, values, selection, seg_lengths):
    tiles = (PARTS, ROWS, HK * DH)
    packed, bias = pl.pallas_call(
        pack_kernel,
        out_shape=(
            jax.ShapeDtypeStruct((DEV, MESSAGE, DH), jnp.bfloat16),
            jax.ShapeDtypeStruct((BLOCK, TOPK * BLOCK), jnp.float32),
        ),
        in_specs=[hbm()] * 4,
        out_specs=(vmem(), vmem()),
        scratch_shapes=[
            pltpu.SMEM((1, TOPK), jnp.int32),
            pltpu.SMEM((NSEG,), jnp.int32),
            pltpu.SemaphoreType.DMA((UNITS + 2,)),
        ],
        compiler_params=params(),
        name="pack",
    )(in_hbm(selection), in_hbm(seg_lengths), in_hbm(keys.reshape(tiles)), in_hbm(values.reshape(tiles)))
    table = lax.all_to_all(packed, AXES, 0, 0, tiled=True)
    picks = table[:, ROWS, :REMOTE].astype(jnp.int32).reshape(DEV * REMOTE)
    shares = pl.pallas_call(
        gather_kernel,
        out_shape=jax.ShapeDtypeStruct((DEV, REMOTE, ROWS, DH), jnp.bfloat16),
        in_specs=[smem(), vmem()],
        out_specs=vmem(),
        compiler_params=params(),
        name="pick",
    )(picks, table)
    got = lax.all_to_all(shares, AXES, 0, 0, tiled=True)
    return pl.pallas_call(
        attend_kernel,
        out_shape=jax.ShapeDtypeStruct((BLOCK, HQ * DH), jnp.bfloat16),
        in_specs=[vmem()] * 5,
        out_specs=vmem(),
        compiler_params=params(),
        name="attend",
    )(queries, keys, values, bias, got)


def solution(mesh):
    return jax.shard_map(
        body,
        mesh=mesh,
        in_specs=(P(AXES, None), P(AXES, None), P(AXES, None), P(AXES, None), P()),
        out_specs=P(AXES, None),
        check_vma=False,
    )
```

```python
import jax
import jax.numpy as jnp
from jax import lax
from jax.experimental import pallas as pl
from jax.experimental.pallas import tpu as pltpu
from jax.sharding import Mesh
from jax.sharding import PartitionSpec as P

HQ = 40
HK = 8
DH = 128
BLOCK = 128
TOPK = 8
NSEG = 8
GROUP = HQ // HK
REMOTE = TOPK - 1
DEV = 128
ROWS = 16
PARTS = BLOCK // ROWS
UNITS = 2 * HK
EXTRA = 2
MESSAGE = ROWS + EXTRA
AXES = ("y_lo", "core", "x", "y_hi", "z")
SIZES = (2, 2, 4, 2, 4)
ORDER = ("z", "x", "y_lo", "y_hi", "core")
SCALE = DH**-0.5
LOG2E = 1.4426950408889634
FILL = -1e30


def own_block():
    block = jnp.int32(0)
    for axis, size in zip(AXES, SIZES):
        block = block * size + lax.axis_index(axis)
    return block


def place(block):
    at = {}
    for axis, size in zip(reversed(AXES), reversed(SIZES)):
        at[axis] = block & (size - 1)
        block = block >> (size.bit_length() - 1)
    where = jnp.int32(0)
    for axis in ORDER:
        where = where * SIZES[AXES.index(axis)] + at[axis]
    return where


def remote_picks(sel_ref, me):
    picks = []
    passed = jnp.int32(0)
    for slot in range(REMOTE):
        passed = jnp.where(sel_ref[0, slot] == me, 1, passed)
        picks.append(jnp.where(passed == 1, sel_ref[0, slot + 1], sel_ref[0, slot]))
    return picks


def pack_kernel(sel_hbm, len_hbm, k_hbm, v_hbm, out_ref, bias_ref, sel_ref, len_ref, k_ref, v_ref, sems):
    scalars = [
        pltpu.make_async_copy(sel_hbm, sel_ref, sems.at[0]),
        pltpu.make_async_copy(len_hbm, len_ref, sems.at[1]),
    ]
    tokens = [
        pltpu.make_async_copy(k_hbm, k_ref, sems.at[2]),
        pltpu.make_async_copy(v_hbm, v_ref, sems.at[3]),
    ]
    for copy in scalars + tokens:
        copy.start()
    for copy in scalars:
        copy.wait()
    me = own_block()
    picks = remote_picks(sel_ref, me)
    lane = lax.broadcasted_iota(jnp.int32, (EXTRA, BLOCK), 1)
    row = jnp.zeros((EXTRA, BLOCK), jnp.int32)
    for slot in range(REMOTE):
        row = jnp.where(lane == slot, place(picks[slot]), row)
    extra = row.astype(jnp.float32).astype(jnp.bfloat16)
    row = lax.broadcasted_iota(jnp.int32, (BLOCK, BLOCK), 0) + me * BLOCK
    lane = lax.broadcasted_iota(jnp.int32, (BLOCK, BLOCK), 1)
    start = jnp.zeros((BLOCK, BLOCK), jnp.int32)
    end = jnp.int32(0)
    for seg in range(NSEG):
        end = end + len_ref[seg]
        start = jnp.where(row >= end, end, start)
    for slot, block in enumerate([me] + picks):
        pos = lane + block * BLOCK
        allowed = (pos <= row) & (pos >= start)
        bias_ref[:, slot * BLOCK : (slot + 1) * BLOCK] = jnp.where(allowed, 0.0, FILL)
    for copy in tokens:
        copy.wait()
    for unit in range(UNITS):
        src = k_ref if unit < HK else v_ref
        col = (unit % HK) * DH
        for part in range(PARTS):
            at = (unit * PARTS + part) * MESSAGE
            out_ref[at : at + ROWS, :] = src[part * ROWS : (part + 1) * ROWS, col : col + DH]
            out_ref[at + ROWS : at + MESSAGE, :] = extra


def gather_kernel(picks_ref, table_ref, out_ref, share_ref):
    for block in range(DEV):
        share_ref[block] = table_ref[block * MESSAGE : block * MESSAGE + ROWS, :]

    @pl.loop(0, DEV, unroll=8)
    def _(dest):
        for slot in range(REMOTE):
            block = picks_ref[dest * REMOTE + slot]
            out_ref[dest, slot] = share_ref[block]


def attend_kernel(q_ref, k_ref, v_ref, bias_ref, got_ref, out_ref):
    for head in range(HK):
        col = head * DH

        def stacked(own, unit):
            parts = [own[:, col : col + DH]]
            for slot in range(REMOTE):
                share = got_ref[unit * PARTS : (unit + 1) * PARTS, slot]
                parts.append(share.reshape(BLOCK, DH))
            return jnp.concatenate(parts, axis=0)

        keys = stacked(k_ref, head)
        vals = stacked(v_ref, HK + head)
        ones = jnp.ones((TOPK * BLOCK, DH), jnp.bfloat16)
        vals = jnp.concatenate([vals, ones], axis=1)
        for g in range(GROUP):
            qcol = (head * GROUP + g) * DH
            q = q_ref[:, qcol : qcol + DH]
            s = lax.dot_general(q, keys, (((1,), (1,)), ((), ())), preferred_element_type=jnp.float32)
            s = s + bias_ref[...]
            top = jnp.max(s, axis=1, keepdims=True)
            p = jnp.exp2((s - top) * (SCALE * LOG2E)).astype(jnp.bfloat16)
            mixed = jnp.dot(p, vals, preferred_element_type=jnp.float32)
            out_ref[:, qcol : qcol + DH] = (mixed[:, :DH] / mixed[:, DH:]).astype(jnp.bfloat16)


def vmem():
    return pl.BlockSpec(memory_space=pltpu.VMEM)


def hbm():
    return pl.BlockSpec(memory_space=pltpu.HBM)


def smem():
    return pl.BlockSpec(memory_space=pltpu.SMEM)


def params():
    return pltpu.CompilerParams(vmem_limit_bytes=48 * 1024 * 1024)


def in_hbm(x):
    return pltpu.with_memory_space_constraint(x, pltpu.HBM)


def body(queries, keys, values, selection, seg_lengths):
    packed, bias = pl.pallas_call(
        pack_kernel,
        out_shape=(
            jax.ShapeDtypeStruct((DEV * MESSAGE, DH), jnp.bfloat16),
            jax.ShapeDtypeStruct((BLOCK, TOPK * BLOCK), jnp.float32),
        ),
        in_specs=[hbm()] * 4,
        out_specs=(vmem(), vmem()),
        scratch_shapes=[
            pltpu.SMEM((1, TOPK), jnp.int32),
            pltpu.SMEM((NSEG,), jnp.int32),
            pltpu.VMEM((BLOCK, HK * DH), jnp.bfloat16),
            pltpu.VMEM((BLOCK, HK * DH), jnp.bfloat16),
            pltpu.SemaphoreType.DMA((4,)),
        ],
        compiler_params=params(),
        name="pack",
    )(in_hbm(selection), in_hbm(seg_lengths), in_hbm(keys), in_hbm(values))
    packed = packed.reshape(DEV, MESSAGE // EXTRA, EXTRA, DH)
    table = lax.all_to_all(packed, ORDER, 0, 0, tiled=True)
    picks = table[:, ROWS // EXTRA, 0, :REMOTE].astype(jnp.int32).reshape(DEV * REMOTE)
    shares = pl.pallas_call(
        gather_kernel,
        out_shape=jax.ShapeDtypeStruct((DEV, REMOTE, ROWS, DH), jnp.bfloat16),
        in_specs=[smem(), vmem()],
        out_specs=vmem(),
        scratch_shapes=[pltpu.VMEM((DEV, ROWS, DH), jnp.bfloat16)],
        compiler_params=params(),
        name="pick",
    )(picks, table.reshape(DEV * MESSAGE, DH))
    got = lax.all_to_all(shares, ORDER, 0, 0, tiled=True)
    return pl.pallas_call(
        attend_kernel,
        out_shape=jax.ShapeDtypeStruct((BLOCK, HQ * DH), jnp.bfloat16),
        in_specs=[vmem()] * 5,
        out_specs=vmem(),
        compiler_params=params(),
        name="attend",
    )(queries, keys, values, bias, got)


def solution(mesh):
    return jax.shard_map(
        body,
        mesh=Mesh(mesh.devices.reshape(SIZES), AXES),
        in_specs=(P(AXES, None), P(AXES, None), P(AXES, None), P(AXES, None), P()),
        out_specs=P(AXES, None),
        check_vma=False,
    )
```

```python
import jax
import jax.numpy as jnp
from jax import lax
from jax.experimental import pallas as pl
from jax.experimental.pallas import tpu as pltpu
from jax.sharding import Mesh
from jax.sharding import PartitionSpec as P

HQ = 40
HK = 8
DH = 128
BLOCK = 128
TOPK = 8
NSEG = 8
GROUP = HQ // HK
REMOTE = TOPK - 1
DEV = 128
ROWS = 16
PARTS = BLOCK // ROWS
UNITS = 2 * HK
EXTRA = 2
MESSAGE = ROWS + EXTRA
SHARING = BLOCK // TOPK
AXES = ("y_lo", "core", "x", "y_hi", "z")
SIZES = (2, 2, 4, 2, 4)
ORDER = ("z", "x", "y_lo", "y_hi", "core")
SCALE = DH**-0.5
LOG2E = 1.4426950408889634
FILL = -1e30


def own_block():
    block = jnp.int32(0)
    for axis, size in zip(AXES, SIZES):
        block = block * size + lax.axis_index(axis)
    return block


def place(block):
    at = {}
    for axis, size in zip(reversed(AXES), reversed(SIZES)):
        at[axis] = block & (size - 1)
        block = block >> (size.bit_length() - 1)
    where = jnp.int32(0)
    for axis in ORDER:
        where = where * SIZES[AXES.index(axis)] + at[axis]
    return where


def remote_picks(sel_ref, me):
    picks = []
    passed = jnp.int32(0)
    for slot in range(REMOTE):
        passed = jnp.where(sel_ref[0, slot] == me, 1, passed)
        picks.append(jnp.where(passed == 1, sel_ref[0, slot + 1], sel_ref[0, slot]))
    return picks


def pack_kernel(sel_hbm, len_hbm, k_hbm, v_hbm, out_ref, bias_ref, sel_ref, len_ref, k_ref, v_ref, sems):
    scalars = [
        pltpu.make_async_copy(sel_hbm, sel_ref, sems.at[0]),
        pltpu.make_async_copy(len_hbm, len_ref, sems.at[1]),
    ]
    tokens = [
        pltpu.make_async_copy(k_hbm, k_ref, sems.at[2]),
        pltpu.make_async_copy(v_hbm, v_ref, sems.at[3]),
    ]
    for copy in scalars + tokens:
        copy.start()
    for copy in scalars:
        copy.wait()
    me = own_block()
    picks = remote_picks(sel_ref, me)
    lane = lax.broadcasted_iota(jnp.int32, (EXTRA, BLOCK), 1)
    row = jnp.zeros((EXTRA, BLOCK), jnp.int32)
    first = (place(me) & (SHARING - 1)) * TOPK
    for slot in range(REMOTE):
        row = jnp.where(lane == first + slot, place(picks[slot]), row)
    extra = row.astype(jnp.float32).astype(jnp.bfloat16)
    row = lax.broadcasted_iota(jnp.int32, (BLOCK, BLOCK), 0) + me * BLOCK
    lane = lax.broadcasted_iota(jnp.int32, (BLOCK, BLOCK), 1)
    start = jnp.zeros((BLOCK, BLOCK), jnp.int32)
    end = jnp.int32(0)
    for seg in range(NSEG):
        end = end + len_ref[seg]
        start = jnp.where(row >= end, end, start)
    for slot, block in enumerate([me] + picks):
        pos = lane + block * BLOCK
        allowed = (pos <= row) & (pos >= start)
        bias_ref[:, slot * BLOCK : (slot + 1) * BLOCK] = jnp.where(allowed, 0.0, FILL)
    for copy in tokens:
        copy.wait()
    for unit in range(UNITS):
        src = k_ref if unit < HK else v_ref
        col = (unit % HK) * DH
        for part in range(PARTS):
            at = (unit * PARTS + part) * MESSAGE
            out_ref[at : at + ROWS, :] = src[part * ROWS : (part + 1) * ROWS, col : col + DH]
            out_ref[at + ROWS : at + MESSAGE, :] = extra


def gather_kernel(table_ref, out_ref, share_ref, lanes_ref, picks_ref, sem):
    for row in range(DEV // SHARING):
        total = jnp.zeros((EXTRA, BLOCK), jnp.float32)
        for block in range(row * SHARING, (row + 1) * SHARING):
            at = block * MESSAGE + ROWS
            total = total + table_ref[at : at + EXTRA, :].astype(jnp.float32)
        lanes_ref[row : row + 1, :] = total[:1].astype(jnp.int32)
    copy = pltpu.make_async_copy(lanes_ref, picks_ref, sem)
    copy.start()
    for block in range(DEV):
        share_ref[block] = table_ref[block * MESSAGE : block * MESSAGE + ROWS, :]
    copy.wait()

    @pl.loop(0, DEV // SHARING)
    def _(row):
        for column in range(SHARING):
            for slot in range(REMOTE):
                block = picks_ref[row, column * TOPK + slot]
                out_ref[row * SHARING + column, slot] = share_ref[block]


def attend_kernel(q_ref, k_ref, v_ref, bias_ref, got_ref, out_hbm, out_ref, sems):
    copies = []
    for head in range(HK):
        col = head * DH

        def stacked(own, unit):
            parts = [own[:, col : col + DH]]
            for slot in range(REMOTE):
                share = got_ref[unit * PARTS : (unit + 1) * PARTS, slot]
                parts.append(share.reshape(BLOCK, DH))
            return jnp.concatenate(parts, axis=0)

        keys = stacked(k_ref, head)
        vals = stacked(v_ref, HK + head)
        ones = jnp.ones((TOPK * BLOCK, DH), jnp.bfloat16)
        vals = jnp.concatenate([vals, ones], axis=1)
        for g in range(GROUP):
            qcol = (head * GROUP + g) * DH
            q = q_ref[:, qcol : qcol + DH]
            s = lax.dot_general(q, keys, (((1,), (1,)), ((), ())), preferred_element_type=jnp.float32)
            s = s + bias_ref[...]
            top = jnp.max(s, axis=1, keepdims=True)
            p = jnp.exp2((s - top) * (SCALE * LOG2E)).astype(jnp.bfloat16)
            mixed = jnp.dot(p, vals, preferred_element_type=jnp.float32)
            out_ref[:, qcol : qcol + DH] = (mixed[:, :DH] / mixed[:, DH:]).astype(jnp.bfloat16)
        if head % 2 == 1:
            cols = slice((head - 1) * GROUP * DH, (head + 1) * GROUP * DH)
            copies.append(pltpu.make_async_copy(out_ref.at[:, cols], out_hbm.at[:, cols], sems.at[head // 2]))
            copies[-1].start()
    for copy in copies:
        copy.wait()


def vmem():
    return pl.BlockSpec(memory_space=pltpu.VMEM)


def hbm():
    return pl.BlockSpec(memory_space=pltpu.HBM)


def smem():
    return pl.BlockSpec(memory_space=pltpu.SMEM)


def params():
    return pltpu.CompilerParams(vmem_limit_bytes=48 * 1024 * 1024)


def in_hbm(x):
    return pltpu.with_memory_space_constraint(x, pltpu.HBM)


def body(queries, keys, values, selection, seg_lengths):
    packed, bias = pl.pallas_call(
        pack_kernel,
        out_shape=(
            jax.ShapeDtypeStruct((DEV * MESSAGE, DH), jnp.bfloat16),
            jax.ShapeDtypeStruct((BLOCK, TOPK * BLOCK), jnp.float32),
        ),
        in_specs=[hbm()] * 4,
        out_specs=(vmem(), vmem()),
        scratch_shapes=[
            pltpu.SMEM((1, TOPK), jnp.int32),
            pltpu.SMEM((NSEG,), jnp.int32),
            pltpu.VMEM((BLOCK, HK * DH), jnp.bfloat16),
            pltpu.VMEM((BLOCK, HK * DH), jnp.bfloat16),
            pltpu.SemaphoreType.DMA((4,)),
        ],
        compiler_params=params(),
        name="pack",
    )(in_hbm(selection), in_hbm(seg_lengths), in_hbm(keys), in_hbm(values))
    packed = packed.reshape(DEV, MESSAGE // EXTRA, EXTRA, DH)
    table = lax.all_to_all(packed, ORDER, 0, 0, tiled=True)
    shares = pl.pallas_call(
        gather_kernel,
        out_shape=jax.ShapeDtypeStruct((DEV, REMOTE, ROWS, DH), jnp.bfloat16),
        in_specs=[vmem()],
        out_specs=vmem(),
        scratch_shapes=[
            pltpu.VMEM((DEV, ROWS, DH), jnp.bfloat16),
            pltpu.VMEM((DEV // SHARING, BLOCK), jnp.int32),
            pltpu.SMEM((DEV // SHARING, BLOCK), jnp.int32),
            pltpu.SemaphoreType.DMA,
        ],
        compiler_params=params(),
        name="pick",
    )(table.reshape(DEV * MESSAGE, DH))
    got = lax.all_to_all(shares, ORDER, 0, 0, tiled=True)
    return pl.pallas_call(
        attend_kernel,
        out_shape=jax.ShapeDtypeStruct((BLOCK, HQ * DH), jnp.bfloat16),
        in_specs=[vmem()] * 5,
        out_specs=hbm(),
        scratch_shapes=[
            pltpu.VMEM((BLOCK, HQ * DH), jnp.bfloat16),
            pltpu.SemaphoreType.DMA((HK // 2,)),
        ],
        compiler_params=params(),
        name="attend",
    )(queries, keys, values, bias, got)


def solution(mesh):
    return jax.shard_map(
        body,
        mesh=Mesh(mesh.devices.reshape(SIZES), AXES),
        in_specs=(P(AXES, None), P(AXES, None), P(AXES, None), P(AXES, None), P()),
        out_specs=P(AXES, None),
        check_vma=False,
    )
```

```python
import jax
import jax.numpy as jnp
from jax import lax
from jax.experimental import pallas as pl
from jax.experimental.pallas import tpu as pltpu
from jax.sharding import Mesh
from jax.sharding import PartitionSpec as P

HQ = 40
HK = 8
DH = 128
BLOCK = 128
TOPK = 8
NSEG = 8
GROUP = HQ // HK
REMOTE = TOPK - 1
DEV = 128
ROWS = 16
PARTS = BLOCK // ROWS
UNITS = 2 * HK
EXTRA = 2
MESSAGE = ROWS + EXTRA
SHARING = BLOCK // TOPK
AXES = ("y_lo", "core", "x", "y_hi", "z")
SIZES = (2, 2, 4, 2, 4)
ORDER = ("z", "x", "y_lo", "y_hi", "core")
SCALE = DH**-0.5
LOG2E = 1.4426950408889634
FILL = -1e30


def own_block():
    block = jnp.int32(0)
    for axis, size in zip(AXES, SIZES):
        block = block * size + lax.axis_index(axis)
    return block


def place(block):
    at = {}
    for axis, size in zip(reversed(AXES), reversed(SIZES)):
        at[axis] = block & (size - 1)
        block = block >> (size.bit_length() - 1)
    where = jnp.int32(0)
    for axis in ORDER:
        where = where * SIZES[AXES.index(axis)] + at[axis]
    return where


def remote_picks(sel_ref, me):
    picks = []
    passed = jnp.int32(0)
    for slot in range(REMOTE):
        passed = jnp.where(sel_ref[0, slot] == me, 1, passed)
        picks.append(jnp.where(passed == 1, sel_ref[0, slot + 1], sel_ref[0, slot]))
    return picks


def pack_kernel(sel_hbm, len_hbm, k_hbm, v_hbm, out_ref, bias_ref, sel_ref, len_ref, k_ref, v_ref, sems):
    scalars = [
        pltpu.make_async_copy(sel_hbm, sel_ref, sems.at[0]),
        pltpu.make_async_copy(len_hbm, len_ref, sems.at[1]),
    ]
    tokens = [
        pltpu.make_async_copy(k_hbm, k_ref, sems.at[2]),
        pltpu.make_async_copy(v_hbm, v_ref, sems.at[3]),
    ]
    for copy in scalars + tokens:
        copy.start()
    for copy in scalars:
        copy.wait()
    me = own_block()
    picks = remote_picks(sel_ref, me)
    lane = lax.broadcasted_iota(jnp.int32, (EXTRA, BLOCK), 1)
    row = jnp.zeros((EXTRA, BLOCK), jnp.int32)
    first = (place(me) & (SHARING - 1)) * TOPK
    for slot in range(REMOTE):
        row = jnp.where(lane == first + slot, place(picks[slot]), row)
    extra = row.astype(jnp.float32).astype(jnp.bfloat16)
    row = lax.broadcasted_iota(jnp.int32, (BLOCK, BLOCK), 0) + me * BLOCK
    lane = lax.broadcasted_iota(jnp.int32, (BLOCK, BLOCK), 1)
    start = jnp.zeros((BLOCK, BLOCK), jnp.int32)
    end = jnp.int32(0)
    for seg in range(NSEG):
        end = end + len_ref[seg]
        start = jnp.where(row >= end, end, start)
    for slot, block in enumerate([me] + picks):
        pos = lane + block * BLOCK
        allowed = (pos <= row) & (pos >= start)
        bias_ref[:, slot * BLOCK : (slot + 1) * BLOCK] = jnp.where(allowed, 0.0, FILL)
    for copy in tokens:
        copy.wait()
    for unit in range(UNITS):
        src = k_ref if unit < HK else v_ref
        col = (unit % HK) * DH
        for part in range(PARTS):
            at = (unit * PARTS + part) * MESSAGE
            out_ref[at : at + ROWS, :] = src[part * ROWS : (part + 1) * ROWS, col : col + DH]
            out_ref[at + ROWS : at + MESSAGE, :] = extra


def gather_kernel(table_ref, out_ref, share_ref, lanes_ref, picks_ref, sem):
    for row in range(DEV // SHARING):
        total = jnp.zeros((EXTRA, BLOCK), jnp.float32)
        for block in range(row * SHARING, (row + 1) * SHARING):
            at = block * MESSAGE + ROWS
            total = total + table_ref[at : at + EXTRA, :].astype(jnp.float32)
        lanes_ref[row : row + 1, :] = total[:1].astype(jnp.int32)
    copy = pltpu.make_async_copy(lanes_ref, picks_ref, sem)
    copy.start()
    for block in range(DEV):
        share_ref[block] = table_ref[block * MESSAGE : block * MESSAGE + ROWS, :]
    copy.wait()

    for dest in range(DEV):
        row, first = dest // SHARING, dest % SHARING * TOPK
        blocks = [picks_ref[row, first + slot] for slot in range(REMOTE)]
        shares = [share_ref[block] for block in blocks]
        for slot in range(REMOTE):
            out_ref[dest, slot] = shares[slot]


def attend_kernel(q_ref, k_ref, v_ref, bias_ref, got_ref, out_hbm, out_ref, sems):
    copies = []
    for head in range(HK):
        col = head * DH

        def stacked(own, unit):
            parts = [own[:, col : col + DH]]
            for slot in range(REMOTE):
                share = got_ref[unit * PARTS : (unit + 1) * PARTS, slot]
                parts.append(share.reshape(BLOCK, DH))
            return jnp.concatenate(parts, axis=0)

        keys = stacked(k_ref, head)
        vals = stacked(v_ref, HK + head)
        ones = jnp.ones((TOPK * BLOCK, DH), jnp.bfloat16)
        vals = jnp.concatenate([vals, ones], axis=1)
        for g in range(GROUP):
            qcol = (head * GROUP + g) * DH
            q = q_ref[:, qcol : qcol + DH]
            s = lax.dot_general(q, keys, (((1,), (1,)), ((), ())), preferred_element_type=jnp.float32)
            s = s + bias_ref[...]
            top = jnp.max(s, axis=1, keepdims=True)
            p = jnp.exp2((s - top) * (SCALE * LOG2E)).astype(jnp.bfloat16)
            mixed = jnp.dot(p, vals, preferred_element_type=jnp.float32)
            out_ref[:, qcol : qcol + DH] = (mixed[:, :DH] / mixed[:, DH:]).astype(jnp.bfloat16)
        if head % 2 == 1:
            cols = slice((head - 1) * GROUP * DH, (head + 1) * GROUP * DH)
            copies.append(pltpu.make_async_copy(out_ref.at[:, cols], out_hbm.at[:, cols], sems.at[head // 2]))
            copies[-1].start()
    for copy in copies:
        copy.wait()


def vmem():
    return pl.BlockSpec(memory_space=pltpu.VMEM)


def hbm():
    return pl.BlockSpec(memory_space=pltpu.HBM)


def smem():
    return pl.BlockSpec(memory_space=pltpu.SMEM)


def params():
    return pltpu.CompilerParams(vmem_limit_bytes=48 * 1024 * 1024)


def in_hbm(x):
    return pltpu.with_memory_space_constraint(x, pltpu.HBM)


def body(queries, keys, values, selection, seg_lengths):
    packed, bias = pl.pallas_call(
        pack_kernel,
        out_shape=(
            jax.ShapeDtypeStruct((DEV * MESSAGE, DH), jnp.bfloat16),
            jax.ShapeDtypeStruct((BLOCK, TOPK * BLOCK), jnp.float32),
        ),
        in_specs=[hbm()] * 4,
        out_specs=(vmem(), vmem()),
        scratch_shapes=[
            pltpu.SMEM((1, TOPK), jnp.int32),
            pltpu.SMEM((NSEG,), jnp.int32),
            pltpu.VMEM((BLOCK, HK * DH), jnp.bfloat16),
            pltpu.VMEM((BLOCK, HK * DH), jnp.bfloat16),
            pltpu.SemaphoreType.DMA((4,)),
        ],
        compiler_params=params(),
        name="pack",
    )(in_hbm(selection), in_hbm(seg_lengths), in_hbm(keys), in_hbm(values))
    packed = packed.reshape(DEV, MESSAGE // EXTRA, EXTRA, DH)
    table = lax.all_to_all(packed, ORDER, 0, 0, tiled=True)
    shares = pl.pallas_call(
        gather_kernel,
        out_shape=jax.ShapeDtypeStruct((DEV, REMOTE, ROWS, DH), jnp.bfloat16),
        in_specs=[vmem()],
        out_specs=vmem(),
        scratch_shapes=[
            pltpu.VMEM((DEV, ROWS, DH), jnp.bfloat16),
            pltpu.VMEM((DEV // SHARING, BLOCK), jnp.int32),
            pltpu.SMEM((DEV // SHARING, BLOCK), jnp.int32),
            pltpu.SemaphoreType.DMA,
        ],
        compiler_params=params(),
        name="pick",
    )(table.reshape(DEV * MESSAGE, DH))
    got = lax.all_to_all(shares, ORDER, 0, 0, tiled=True)
    return pl.pallas_call(
        attend_kernel,
        out_shape=jax.ShapeDtypeStruct((BLOCK, HQ * DH), jnp.bfloat16),
        in_specs=[vmem()] * 5,
        out_specs=hbm(),
        scratch_shapes=[
            pltpu.VMEM((BLOCK, HQ * DH), jnp.bfloat16),
            pltpu.SemaphoreType.DMA((HK // 2,)),
        ],
        compiler_params=params(),
        name="attend",
    )(queries, keys, values, bias, got)


def solution(mesh):
    return jax.shard_map(
        body,
        mesh=Mesh(mesh.devices.reshape(SIZES), AXES),
        in_specs=(P(AXES, None), P(AXES, None), P(AXES, None), P(AXES, None), P()),
        out_specs=P(AXES, None),
        check_vma=False,
    )
```

```python
import jax
import jax.numpy as jnp
from jax import lax
from jax.experimental import pallas as pl
from jax.experimental.pallas import tpu as pltpu
from jax.sharding import Mesh
from jax.sharding import PartitionSpec as P

HQ = 40
HK = 8
DH = 128
BLOCK = 128
TOPK = 8
NSEG = 8
GROUP = HQ // HK
REMOTE = TOPK - 1
DEV = 128
ROWS = 16
PARTS = BLOCK // ROWS
UNITS = 2 * HK
EXTRA = 2
MESSAGE = ROWS + EXTRA
SHARING = BLOCK // TOPK
AXES = ("y_lo", "core", "x", "y_hi", "z")
SIZES = (2, 2, 4, 2, 4)
ORDER = ("z", "x", "y_lo", "y_hi", "core")
SCALE = DH**-0.5
LOG2E = 1.4426950408889634
FILL = -1e30


def own_block():
    block = jnp.int32(0)
    for axis, size in zip(AXES, SIZES):
        block = block * size + lax.axis_index(axis)
    return block


def place(block):
    at = {}
    for axis, size in zip(reversed(AXES), reversed(SIZES)):
        at[axis] = block & (size - 1)
        block = block >> (size.bit_length() - 1)
    where = jnp.int32(0)
    for axis in ORDER:
        where = where * SIZES[AXES.index(axis)] + at[axis]
    return where


def remote_picks(sel_ref, me):
    picks = []
    passed = jnp.int32(0)
    for slot in range(REMOTE):
        passed = jnp.where(sel_ref[0, slot] == me, 1, passed)
        picks.append(jnp.where(passed == 1, sel_ref[0, slot + 1], sel_ref[0, slot]))
    return picks


def pack_kernel(sel_hbm, len_hbm, k_hbm, v_hbm, out_ref, bias_ref, turned_ref, sel_ref, len_ref, k_ref, v_ref, sems):
    scalars = [
        pltpu.make_async_copy(sel_hbm, sel_ref, sems.at[0]),
        pltpu.make_async_copy(len_hbm, len_ref, sems.at[1]),
    ]
    tokens = [
        pltpu.make_async_copy(k_hbm, k_ref, sems.at[2]),
        pltpu.make_async_copy(v_hbm, v_ref, sems.at[3]),
    ]
    for copy in scalars + tokens:
        copy.start()
    for copy in scalars:
        copy.wait()
    me = own_block()
    picks = remote_picks(sel_ref, me)
    lane = lax.broadcasted_iota(jnp.int32, (EXTRA, BLOCK), 1)
    row = jnp.zeros((EXTRA, BLOCK), jnp.int32)
    first = (place(me) & (SHARING - 1)) * TOPK
    for slot in range(REMOTE):
        row = jnp.where(lane == first + slot, place(picks[slot]), row)
    extra = row.astype(jnp.float32).astype(jnp.bfloat16)
    row = lax.broadcasted_iota(jnp.int32, (BLOCK, BLOCK), 0) + me * BLOCK
    lane = lax.broadcasted_iota(jnp.int32, (BLOCK, BLOCK), 1)
    start = jnp.zeros((BLOCK, BLOCK), jnp.int32)
    end = jnp.int32(0)
    for seg in range(NSEG):
        end = end + len_ref[seg]
        start = jnp.where(row >= end, end, start)
    for slot, block in enumerate([me] + picks):
        pos = lane + block * BLOCK
        allowed = (pos <= row) & (pos >= start)
        bias_ref[:, slot * BLOCK : (slot + 1) * BLOCK] = jnp.where(allowed, 0.0, FILL).astype(jnp.bfloat16)
    for copy in tokens:
        copy.wait()
    for unit in range(UNITS):
        col = (unit % HK) * DH
        if unit < HK:
            tile = k_ref[:, col : col + DH].T
            turned_ref[col : col + DH, :] = tile
        else:
            tile = v_ref[:, col : col + DH]
        for part in range(PARTS):
            at = (unit * PARTS + part) * MESSAGE
            out_ref[at : at + ROWS, :] = tile[part * ROWS : (part + 1) * ROWS, :]
            out_ref[at + ROWS : at + MESSAGE, :] = extra


def gather_kernel(table_ref, out_ref, share_ref, lanes_ref, picks_ref, sem):
    for row in range(DEV // SHARING):
        total = jnp.zeros((EXTRA, BLOCK), jnp.float32)
        for block in range(row * SHARING, (row + 1) * SHARING):
            at = block * MESSAGE + ROWS
            total = total + table_ref[at : at + EXTRA, :].astype(jnp.float32)
        lanes_ref[row : row + 1, :] = total[:1].astype(jnp.int32)
    copy = pltpu.make_async_copy(lanes_ref, picks_ref, sem)
    copy.start()
    for block in range(DEV):
        share_ref[block] = table_ref[block * MESSAGE : block * MESSAGE + ROWS, :]
    copy.wait()

    for dest in range(DEV):
        row, first = dest // SHARING, dest % SHARING * TOPK
        blocks = [picks_ref[row, first + slot] for slot in range(REMOTE)]
        shares = [share_ref[block] for block in blocks]
        for slot in range(REMOTE):
            out_ref[dest, slot] = shares[slot]


def attend_kernel(q_ref, turned_ref, v_ref, bias_ref, got_ref, out_hbm, out_ref, sems):
    copies = []
    row = lax.broadcasted_iota(jnp.int32, (BLOCK, BLOCK), 0)
    lane = lax.broadcasted_iota(jnp.int32, (BLOCK, BLOCK), 1)
    identity = jnp.where(row == lane, 1.0, 0.0).astype(jnp.bfloat16)
    ones = jnp.ones((TOPK * BLOCK, DH), jnp.bfloat16)

    def remote(unit):
        return [got_ref[unit * PARTS : (unit + 1) * PARTS, slot].reshape(BLOCK, DH) for slot in range(REMOTE)]

    def operands(head):
        own = slice(head * DH, (head + 1) * DH)
        keys = jnp.concatenate([turned_ref[own, :]] + remote(head), axis=1)
        vals = jnp.concatenate([v_ref[:, own]] + remote(HK + head), axis=0)
        return jnp.concatenate([keys, bias_ref[...]], axis=0), jnp.concatenate([vals, ones], axis=1)

    def scores(index, keys):
        q = jnp.concatenate([q_ref[:, index * DH : (index + 1) * DH], identity], axis=1)
        return jnp.dot(q, keys, preferred_element_type=jnp.float32)

    def finish(index, p, vals):
        mixed = jnp.dot(p, vals, preferred_element_type=jnp.float32)
        out_ref[:, index * DH : (index + 1) * DH] = (mixed[:, :DH] / mixed[:, DH:]).astype(jnp.bfloat16)
        if (index + 1) % (2 * GROUP) == 0:
            cols = slice((index + 1 - 2 * GROUP) * DH, (index + 1) * DH)
            sem = sems.at[index // (2 * GROUP)]
            copies.append(pltpu.make_async_copy(out_ref.at[:, cols], out_hbm.at[:, cols], sem))
            copies[-1].start()

    pairs = [operands(head) for head in range(HK)]
    s = scores(0, pairs[0][0])
    before = None
    for index in range(HQ):
        later = scores(index + 1, pairs[(index + 1) // GROUP][0]) if index + 1 < HQ else None
        top = jnp.max(s, axis=1, keepdims=True)
        p = jnp.exp2((s - top) * (SCALE * LOG2E)).astype(jnp.bfloat16)
        if before is not None:
            finish(*before)
        before = (index, p, pairs[index // GROUP][1])
        s = later
    finish(*before)
    for copy in copies:
        copy.wait()


def vmem():
    return pl.BlockSpec(memory_space=pltpu.VMEM)


def hbm():
    return pl.BlockSpec(memory_space=pltpu.HBM)


def smem():
    return pl.BlockSpec(memory_space=pltpu.SMEM)


def params():
    return pltpu.CompilerParams(vmem_limit_bytes=48 * 1024 * 1024)


def in_hbm(x):
    return pltpu.with_memory_space_constraint(x, pltpu.HBM)


def body(queries, keys, values, selection, seg_lengths):
    packed, bias, turned = pl.pallas_call(
        pack_kernel,
        out_shape=(
            jax.ShapeDtypeStruct((DEV * MESSAGE, DH), jnp.bfloat16),
            jax.ShapeDtypeStruct((BLOCK, TOPK * BLOCK), jnp.bfloat16),
            jax.ShapeDtypeStruct((HK * DH, BLOCK), jnp.bfloat16),
        ),
        in_specs=[hbm()] * 4,
        out_specs=(vmem(), vmem(), vmem()),
        scratch_shapes=[
            pltpu.SMEM((1, TOPK), jnp.int32),
            pltpu.SMEM((NSEG,), jnp.int32),
            pltpu.VMEM((BLOCK, HK * DH), jnp.bfloat16),
            pltpu.VMEM((BLOCK, HK * DH), jnp.bfloat16),
            pltpu.SemaphoreType.DMA((4,)),
        ],
        compiler_params=params(),
        name="pack",
    )(in_hbm(selection), in_hbm(seg_lengths), in_hbm(keys), in_hbm(values))
    packed = packed.reshape(DEV, MESSAGE // EXTRA, EXTRA, DH)
    table = lax.all_to_all(packed, ORDER, 0, 0, tiled=True)
    shares = pl.pallas_call(
        gather_kernel,
        out_shape=jax.ShapeDtypeStruct((DEV, REMOTE, ROWS, DH), jnp.bfloat16),
        in_specs=[vmem()],
        out_specs=vmem(),
        scratch_shapes=[
            pltpu.VMEM((DEV, ROWS, DH), jnp.bfloat16),
            pltpu.VMEM((DEV // SHARING, BLOCK), jnp.int32),
            pltpu.SMEM((DEV // SHARING, BLOCK), jnp.int32),
            pltpu.SemaphoreType.DMA,
        ],
        compiler_params=params(),
        name="pick",
    )(table.reshape(DEV * MESSAGE, DH))
    got = lax.all_to_all(shares, ORDER, 0, 0, tiled=True)
    return pl.pallas_call(
        attend_kernel,
        out_shape=jax.ShapeDtypeStruct((BLOCK, HQ * DH), jnp.bfloat16),
        in_specs=[vmem()] * 5,
        out_specs=hbm(),
        scratch_shapes=[
            pltpu.VMEM((BLOCK, HQ * DH), jnp.bfloat16),
            pltpu.SemaphoreType.DMA((HK // 2,)),
        ],
        compiler_params=params(),
        name="attend",
    )(queries, turned, values, bias, got)


def solution(mesh):
    return jax.shard_map(
        body,
        mesh=Mesh(mesh.devices.reshape(SIZES), AXES),
        in_specs=(P(AXES, None), P(AXES, None), P(AXES, None), P(AXES, None), P()),
        out_specs=P(AXES, None),
        check_vma=False,
    )
```

```python
import jax
import jax.numpy as jnp
from jax import lax
from jax.experimental import pallas as pl
from jax.experimental.pallas import tpu as pltpu
from jax.sharding import Mesh
from jax.sharding import PartitionSpec as P

HQ = 40
HK = 8
DH = 128
BLOCK = 128
TOPK = 8
NSEG = 8
GROUP = HQ // HK
REMOTE = TOPK - 1
DEV = 128
ROWS = 16
PARTS = BLOCK // ROWS
UNITS = 2 * HK
EXTRA = 2
MESSAGE = ROWS + EXTRA
SHARING = BLOCK // TOPK
AXES = ("y_lo", "core", "x", "y_hi", "z")
SIZES = (2, 2, 4, 2, 4)
ORDER = ("z", "x", "y_lo", "y_hi", "core")
SCALE = DH**-0.5
LOG2E = 1.4426950408889634
FILL = -1e30


def own_block():
    block = jnp.int32(0)
    for axis, size in zip(AXES, SIZES):
        block = block * size + lax.axis_index(axis)
    return block


def place(block):
    at = {}
    for axis, size in zip(reversed(AXES), reversed(SIZES)):
        at[axis] = block & (size - 1)
        block = block >> (size.bit_length() - 1)
    where = jnp.int32(0)
    for axis in ORDER:
        where = where * SIZES[AXES.index(axis)] + at[axis]
    return where


def remote_picks(sel_ref, me):
    picks = []
    passed = jnp.int32(0)
    for slot in range(REMOTE):
        passed = jnp.where(sel_ref[0, slot] == me, 1, passed)
        picks.append(jnp.where(passed == 1, sel_ref[0, slot + 1], sel_ref[0, slot]))
    return picks


def pack_kernel(sel_hbm, len_hbm, k_hbm, v_hbm, out_ref, bias_ref, turned_ref, sel_ref, len_ref, k_ref, v_ref, sems):
    scalars = [
        pltpu.make_async_copy(sel_hbm, sel_ref, sems.at[0]),
        pltpu.make_async_copy(len_hbm, len_ref, sems.at[1]),
    ]
    tokens = [
        pltpu.make_async_copy(k_hbm, k_ref, sems.at[2]),
        pltpu.make_async_copy(v_hbm, v_ref, sems.at[3]),
    ]
    for copy in scalars + tokens:
        copy.start()
    for copy in scalars:
        copy.wait()
    me = own_block()
    picks = remote_picks(sel_ref, me)
    lane = lax.broadcasted_iota(jnp.int32, (EXTRA, BLOCK), 1)
    row = jnp.zeros((EXTRA, BLOCK), jnp.int32)
    first = (place(me) & (SHARING - 1)) * TOPK
    for slot in range(REMOTE):
        row = jnp.where(lane == first + slot, place(picks[slot]), row)
    extra = row.astype(jnp.float32).astype(jnp.bfloat16)
    row = lax.broadcasted_iota(jnp.int32, (BLOCK, BLOCK), 0) + me * BLOCK
    lane = lax.broadcasted_iota(jnp.int32, (BLOCK, BLOCK), 1)
    start = jnp.zeros((BLOCK, BLOCK), jnp.int32)
    end = jnp.int32(0)
    for seg in range(NSEG):
        end = end + len_ref[seg]
        start = jnp.where(row >= end, end, start)
    for slot, block in enumerate([me] + picks):
        pos = lane + block * BLOCK
        allowed = (pos <= row) & (pos >= start)
        bias_ref[:, slot * BLOCK : (slot + 1) * BLOCK] = jnp.where(allowed, 0.0, FILL).astype(jnp.bfloat16)
    for unit in range(UNITS):
        if unit % HK == 0:
            tokens[unit // HK].wait()
        col = (unit % HK) * DH
        if unit < HK:
            tile = k_ref[:, col : col + DH].T
            turned_ref[col : col + DH, :] = tile
        else:
            tile = v_ref[:, col : col + DH]
        for part in range(PARTS):
            at = (unit * PARTS + part) * MESSAGE
            out_ref[at : at + ROWS, :] = tile[part * ROWS : (part + 1) * ROWS, :]
            out_ref[at + ROWS : at + MESSAGE, :] = extra


def gather_kernel(table_ref, out_ref, share_ref, lanes_ref, picks_ref, sem):
    for row in range(DEV // SHARING):
        total = jnp.zeros((EXTRA, BLOCK), jnp.float32)
        for block in range(row * SHARING, (row + 1) * SHARING):
            at = block * MESSAGE + ROWS
            total = total + table_ref[at : at + EXTRA, :].astype(jnp.float32)
        lanes_ref[row : row + 1, :] = total[:1].astype(jnp.int32)
    copy = pltpu.make_async_copy(lanes_ref, picks_ref, sem)
    copy.start()
    for block in range(DEV):
        share_ref[block] = table_ref[block * MESSAGE : block * MESSAGE + ROWS, :]
    copy.wait()

    for dest in range(DEV):
        row, first = dest // SHARING, dest % SHARING * TOPK
        blocks = [picks_ref[row, first + slot] for slot in range(REMOTE)]
        shares = [share_ref[block] for block in blocks]
        for slot in range(REMOTE):
            out_ref[dest, slot] = shares[slot]


def attend_kernel(q_ref, turned_ref, v_ref, bias_ref, got_ref, out_hbm, out_ref, sems):
    copies = []
    ends = [16, 28, 36, HQ]
    row = lax.broadcasted_iota(jnp.int32, (BLOCK, BLOCK), 0)
    lane = lax.broadcasted_iota(jnp.int32, (BLOCK, BLOCK), 1)
    identity = jnp.where(row == lane, 1.0, 0.0).astype(jnp.bfloat16)
    ones = jnp.ones((TOPK * BLOCK, DH), jnp.bfloat16)

    def remote(unit):
        return [got_ref[unit * PARTS : (unit + 1) * PARTS, slot].reshape(BLOCK, DH) for slot in range(REMOTE)]

    def operands(head):
        own = slice(head * DH, (head + 1) * DH)
        keys = jnp.concatenate([turned_ref[own, :]] + remote(head), axis=1)
        vals = jnp.concatenate([v_ref[:, own]] + remote(HK + head), axis=0)
        return jnp.concatenate([keys, bias_ref[...]], axis=0), jnp.concatenate([vals, ones], axis=1)

    def scores(index, keys):
        q = jnp.concatenate([q_ref[:, index * DH : (index + 1) * DH], identity], axis=1)
        return jnp.dot(q, keys, preferred_element_type=jnp.float32)

    def finish(index, p, vals):
        mixed = jnp.dot(p, vals, preferred_element_type=jnp.float32)
        out_ref[:, index * DH : (index + 1) * DH] = (mixed[:, :DH] / mixed[:, DH:]).astype(jnp.bfloat16)
        if index + 1 in ends:
            part = ends.index(index + 1)
            cols = slice(ends[part - 1] * DH if part else 0, (index + 1) * DH)
            copies.append(pltpu.make_async_copy(out_ref.at[:, cols], out_hbm.at[:, cols], sems.at[part]))
            copies[-1].start()

    pairs = [operands(head) for head in range(HK)]
    s = scores(0, pairs[0][0])
    before = None
    for index in range(HQ):
        later = scores(index + 1, pairs[(index + 1) // GROUP][0]) if index + 1 < HQ else None
        top = jnp.max(s, axis=1, keepdims=True)
        p = jnp.exp2((s - top) * (SCALE * LOG2E)).astype(jnp.bfloat16)
        if before is not None:
            finish(*before)
        before = (index, p, pairs[index // GROUP][1])
        s = later
    finish(*before)
    for copy in copies:
        copy.wait()


def vmem():
    return pl.BlockSpec(memory_space=pltpu.VMEM)


def hbm():
    return pl.BlockSpec(memory_space=pltpu.HBM)


def smem():
    return pl.BlockSpec(memory_space=pltpu.SMEM)


def params():
    return pltpu.CompilerParams(vmem_limit_bytes=48 * 1024 * 1024)


def in_hbm(x):
    return pltpu.with_memory_space_constraint(x, pltpu.HBM)


def body(queries, keys, values, selection, seg_lengths):
    packed, bias, turned = pl.pallas_call(
        pack_kernel,
        out_shape=(
            jax.ShapeDtypeStruct((DEV * MESSAGE, DH), jnp.bfloat16),
            jax.ShapeDtypeStruct((BLOCK, TOPK * BLOCK), jnp.bfloat16),
            jax.ShapeDtypeStruct((HK * DH, BLOCK), jnp.bfloat16),
        ),
        in_specs=[hbm()] * 4,
        out_specs=(vmem(), vmem(), vmem()),
        scratch_shapes=[
            pltpu.SMEM((1, TOPK), jnp.int32),
            pltpu.SMEM((NSEG,), jnp.int32),
            pltpu.VMEM((BLOCK, HK * DH), jnp.bfloat16),
            pltpu.VMEM((BLOCK, HK * DH), jnp.bfloat16),
            pltpu.SemaphoreType.DMA((4,)),
        ],
        compiler_params=params(),
        name="pack",
    )(in_hbm(selection), in_hbm(seg_lengths), in_hbm(keys), in_hbm(values))
    packed = packed.reshape(DEV, MESSAGE // EXTRA, EXTRA, DH)
    table = lax.all_to_all(packed, ORDER, 0, 0, tiled=True)
    shares = pl.pallas_call(
        gather_kernel,
        out_shape=jax.ShapeDtypeStruct((DEV, REMOTE, ROWS, DH), jnp.bfloat16),
        in_specs=[vmem()],
        out_specs=vmem(),
        scratch_shapes=[
            pltpu.VMEM((DEV, ROWS, DH), jnp.bfloat16),
            pltpu.VMEM((DEV // SHARING, BLOCK), jnp.int32),
            pltpu.SMEM((DEV // SHARING, BLOCK), jnp.int32),
            pltpu.SemaphoreType.DMA,
        ],
        compiler_params=params(),
        name="pick",
    )(table.reshape(DEV * MESSAGE, DH))
    got = lax.all_to_all(shares, ORDER, 0, 0, tiled=True)
    return pl.pallas_call(
        attend_kernel,
        out_shape=jax.ShapeDtypeStruct((BLOCK, HQ * DH), jnp.bfloat16),
        in_specs=[vmem()] * 5,
        out_specs=hbm(),
        scratch_shapes=[
            pltpu.VMEM((BLOCK, HQ * DH), jnp.bfloat16),
            pltpu.SemaphoreType.DMA((HK // 2,)),
        ],
        compiler_params=params(),
        name="attend",
    )(queries, turned, values, bias, got)


def solution(mesh):
    return jax.shard_map(
        body,
        mesh=Mesh(mesh.devices.reshape(SIZES), AXES),
        in_specs=(P(AXES, None), P(AXES, None), P(AXES, None), P(AXES, None), P()),
        out_specs=P(AXES, None),
        check_vma=False,
    )
```

```python
import jax
import jax.numpy as jnp
from jax import lax
from jax.experimental import pallas as pl
from jax.experimental.pallas import tpu as pltpu
from jax.sharding import Mesh
from jax.sharding import PartitionSpec as P

HQ = 40
HK = 8
DH = 128
BLOCK = 128
TOPK = 8
NSEG = 8
GROUP = HQ // HK
REMOTE = TOPK - 1
DEV = 128
ROWS = 16
PARTS = BLOCK // ROWS
UNITS = 2 * HK
EXTRA = 2
MESSAGE = ROWS + EXTRA
SHARING = BLOCK // TOPK
AXES = ("y_lo", "core", "x", "y_hi", "z")
SIZES = (2, 2, 4, 2, 4)
ORDER = ("z", "x", "y_lo", "y_hi", "core")
SCALE = DH**-0.5
LOG2E = 1.4426950408889634
FILL = -1e30


def own_block():
    block = jnp.int32(0)
    for axis, size in zip(AXES, SIZES):
        block = block * size + lax.axis_index(axis)
    return block


def place(block):
    at = {}
    for axis, size in zip(reversed(AXES), reversed(SIZES)):
        at[axis] = block & (size - 1)
        block = block >> (size.bit_length() - 1)
    where = jnp.int32(0)
    for axis in ORDER:
        where = where * SIZES[AXES.index(axis)] + at[axis]
    return where


def remote_picks(sel_ref, me):
    picks = []
    passed = jnp.int32(0)
    for slot in range(REMOTE):
        passed = jnp.where(sel_ref[0, slot] == me, 1, passed)
        picks.append(jnp.where(passed == 1, sel_ref[0, slot + 1], sel_ref[0, slot]))
    return picks


def pack_kernel(sel_hbm, len_hbm, k_hbm, v_hbm, out_ref, bias_ref, turned_ref, sel_ref, len_ref, k_ref, v_ref, sems):
    scalars = [
        pltpu.make_async_copy(sel_hbm, sel_ref, sems.at[0]),
        pltpu.make_async_copy(len_hbm, len_ref, sems.at[1]),
    ]
    tokens = [
        pltpu.make_async_copy(k_hbm, k_ref, sems.at[2]),
        pltpu.make_async_copy(v_hbm, v_ref, sems.at[3]),
    ]
    for copy in scalars + tokens:
        copy.start()
    for copy in scalars:
        copy.wait()
    me = own_block()
    picks = remote_picks(sel_ref, me)
    lane = lax.broadcasted_iota(jnp.int32, (EXTRA, BLOCK), 1)
    row = jnp.zeros((EXTRA, BLOCK), jnp.int32)
    first = (place(me) & (SHARING - 1)) * TOPK
    for slot in range(REMOTE):
        row = jnp.where(lane == first + slot, place(picks[slot]), row)
    extra = row.astype(jnp.float32).astype(jnp.bfloat16)
    row = lax.broadcasted_iota(jnp.int32, (BLOCK, BLOCK), 0) + me * BLOCK
    lane = lax.broadcasted_iota(jnp.int32, (BLOCK, BLOCK), 1)
    start = jnp.zeros((BLOCK, BLOCK), jnp.int32)
    end = jnp.int32(0)
    for seg in range(NSEG):
        end = end + len_ref[seg]
        start = jnp.where(row >= end, end, start)
    for slot, block in enumerate([me] + picks):
        pos = lane + block * BLOCK
        allowed = (pos <= row) & (pos >= start)
        bias_ref[:, slot * BLOCK : (slot + 1) * BLOCK] = jnp.where(allowed, 0.0, FILL).astype(jnp.bfloat16)
    for unit in range(UNITS):
        if unit % HK == 0:
            tokens[unit // HK].wait()
        col = (unit % HK) * DH
        if unit < HK:
            tile = k_ref[:, col : col + DH].T
            turned_ref[col : col + DH, :] = tile
        else:
            tile = v_ref[:, col : col + DH]
        for part in range(PARTS):
            at = (unit * PARTS + part) * MESSAGE
            out_ref[at : at + ROWS, :] = tile[part * ROWS : (part + 1) * ROWS, :]
            out_ref[at + ROWS : at + MESSAGE, :] = extra


def gather_kernel(table_ref, out_ref, share_ref, lanes_ref, picks_ref, sem):
    for row in range(DEV // SHARING):
        total = jnp.zeros((EXTRA, BLOCK), jnp.float32)
        for block in range(row * SHARING, (row + 1) * SHARING):
            at = block * MESSAGE + ROWS
            total = total + table_ref[at : at + EXTRA, :].astype(jnp.float32)
        lanes_ref[row : row + 1, :] = total[:1].astype(jnp.int32)
    copy = pltpu.make_async_copy(lanes_ref, picks_ref, sem)
    copy.start()
    for block in range(DEV):
        share_ref[block] = table_ref[block * MESSAGE : block * MESSAGE + ROWS, :]
    copy.wait()

    for dest in range(DEV):
        row, first = dest // SHARING, dest % SHARING * TOPK
        blocks = [picks_ref[row, first + slot] for slot in range(REMOTE)]
        shares = [share_ref[block] for block in blocks]
        for slot in range(REMOTE):
            out_ref[dest, slot] = shares[slot]


def attend_kernel(q_ref, turned_ref, v_ref, bias_ref, got_ref, out_hbm, out_ref, sems):
    copies = []
    ends = [16, 28, 36, HQ]
    row = lax.broadcasted_iota(jnp.int32, (BLOCK, BLOCK), 0)
    lane = lax.broadcasted_iota(jnp.int32, (BLOCK, BLOCK), 1)
    identity = jnp.where(row == lane, 1.0, 0.0).astype(jnp.bfloat16)
    ones = jnp.ones((TOPK * BLOCK, DH), jnp.bfloat16)

    def remote(unit):
        return [got_ref[unit * PARTS : (unit + 1) * PARTS, slot].reshape(BLOCK, DH) for slot in range(REMOTE)]

    def operands(head):
        own = slice(head * DH, (head + 1) * DH)
        keys = jnp.concatenate([turned_ref[own, :]] + remote(head), axis=1)
        vals = jnp.concatenate([v_ref[:, own]] + remote(HK + head), axis=0)
        return jnp.concatenate([keys, bias_ref[...]], axis=0), jnp.concatenate([vals, ones], axis=1)

    def scores(index, keys):
        q = jnp.concatenate([q_ref[:, index * DH : (index + 1) * DH], identity], axis=1)
        return jnp.dot(q, keys, preferred_element_type=jnp.float32)

    def finish(index, p, vals):
        mixed = jnp.dot(p, vals, preferred_element_type=jnp.float32)
        out_ref[:, index * DH : (index + 1) * DH] = (mixed[:, :DH] / mixed[:, DH:]).astype(jnp.bfloat16)
        if index + 1 in ends:
            part = ends.index(index + 1)
            cols = slice(ends[part - 1] * DH if part else 0, (index + 1) * DH)
            copies.append(pltpu.make_async_copy(out_ref.at[:, cols], out_hbm.at[:, cols], sems.at[part]))
            copies[-1].start()

    pair = after = operands(0)
    s = scores(0, pair[0])
    before = None
    for index in range(HQ):
        if (index + 1) % GROUP == 0 and index + 1 < HQ:
            after = operands((index + 1) // GROUP)
        later = scores(index + 1, after[0]) if index + 1 < HQ else None
        top = jnp.max(s, axis=1, keepdims=True)
        p = jnp.exp2((s - top) * (SCALE * LOG2E)).astype(jnp.bfloat16)
        if before is not None:
            finish(*before)
        before = (index, p, pair[1])
        s, pair = later, after
    finish(*before)
    for copy in copies:
        copy.wait()


def vmem():
    return pl.BlockSpec(memory_space=pltpu.VMEM)


def hbm():
    return pl.BlockSpec(memory_space=pltpu.HBM)


def smem():
    return pl.BlockSpec(memory_space=pltpu.SMEM)


def params():
    return pltpu.CompilerParams(vmem_limit_bytes=48 * 1024 * 1024)


def in_hbm(x):
    return pltpu.with_memory_space_constraint(x, pltpu.HBM)


def body(queries, keys, values, selection, seg_lengths):
    packed, bias, turned = pl.pallas_call(
        pack_kernel,
        out_shape=(
            jax.ShapeDtypeStruct((DEV * MESSAGE, DH), jnp.bfloat16),
            jax.ShapeDtypeStruct((BLOCK, TOPK * BLOCK), jnp.bfloat16),
            jax.ShapeDtypeStruct((HK * DH, BLOCK), jnp.bfloat16),
        ),
        in_specs=[hbm()] * 4,
        out_specs=(vmem(), vmem(), vmem()),
        scratch_shapes=[
            pltpu.SMEM((1, TOPK), jnp.int32),
            pltpu.SMEM((NSEG,), jnp.int32),
            pltpu.VMEM((BLOCK, HK * DH), jnp.bfloat16),
            pltpu.VMEM((BLOCK, HK * DH), jnp.bfloat16),
            pltpu.SemaphoreType.DMA((4,)),
        ],
        compiler_params=params(),
        name="pack",
    )(in_hbm(selection), in_hbm(seg_lengths), in_hbm(keys), in_hbm(values))
    packed = packed.reshape(DEV, MESSAGE // EXTRA, EXTRA, DH)
    table = lax.all_to_all(packed, ORDER, 0, 0, tiled=True)
    shares = pl.pallas_call(
        gather_kernel,
        out_shape=jax.ShapeDtypeStruct((DEV, REMOTE, ROWS, DH), jnp.bfloat16),
        in_specs=[vmem()],
        out_specs=vmem(),
        scratch_shapes=[
            pltpu.VMEM((DEV, ROWS, DH), jnp.bfloat16),
            pltpu.VMEM((DEV // SHARING, BLOCK), jnp.int32),
            pltpu.SMEM((DEV // SHARING, BLOCK), jnp.int32),
            pltpu.SemaphoreType.DMA,
        ],
        compiler_params=params(),
        name="pick",
    )(table.reshape(DEV * MESSAGE, DH))
    got = lax.all_to_all(shares, ORDER, 0, 0, tiled=True)
    return pl.pallas_call(
        attend_kernel,
        out_shape=jax.ShapeDtypeStruct((BLOCK, HQ * DH), jnp.bfloat16),
        in_specs=[vmem()] * 5,
        out_specs=hbm(),
        scratch_shapes=[
            pltpu.VMEM((BLOCK, HQ * DH), jnp.bfloat16),
            pltpu.SemaphoreType.DMA((HK // 2,)),
        ],
        compiler_params=params(),
        name="attend",
    )(queries, turned, values, bias, got)


def solution(mesh):
    return jax.shard_map(
        body,
        mesh=Mesh(mesh.devices.reshape(SIZES), AXES),
        in_specs=(P(AXES, None), P(AXES, None), P(AXES, None), P(AXES, None), P()),
        out_specs=P(AXES, None),
        check_vma=False,
    )
```
